32 devices in a mesh: db: 8 (over z, y), section: 2 (over core), mp: 2 (over x).
Axes of the slice: x: 2, y: 2, z: 4, core: 2. Of those that a mesh axis runs over, the one named last changes fastest.
Arguments:
- hidden_in: bfloat16 [4096, 4096], P('db', 'mp'), may hold values from -24 to 24
- database: bfloat16 [32, 128, 896], P('db'), may hold values from -8.5 to 8.5
- neighbour_ids: int32 [64, 2], replicated, may hold values from 0 to 31, as said below
- enc_gain: float32 [896], replicated, may hold values from 0.1 to 1.9
- enc_up: bfloat16 [896, 2048], P(None, ('section', 'mp')), may hold values from -0.1875 to 0.1875
- enc_down: bfloat16 [2048, 896], P(('section', 'mp')), may hold values from -0.125 to 0.125
- dec_gain: float32 [2, 4096], P('section'), may hold values from 0.1 to 1.9
- w_query: bfloat16 [2, 4096, 2048], P('section', None, 'mp'), may hold values from -0.06328125 to 0.06328125
- w_key: bfloat16 [2, 896, 2048], P('section', None, 'mp'), may hold values from -0.135301004 to 0.135301004
- w_value: bfloat16 [2, 896, 2048], P('section', None, 'mp'), may hold values from -0.1875 to 0.1875
- w_out: bfloat16 [2, 2048, 4096], P('section', 'mp'), may hold values from -0.125 to 0.125
Outputs:
- hidden_out: bfloat16 [4096, 4096], P(('db', 'section'), 'mp')
The draws below stay inside these ranges and needn't reach their ends.
Inputs may be any that keep to these rules, and one draw needn't show every extreme that they name: `neighbour_ids`: block id b is held by db index b // 4. The 16 ids in the rows of one db index name at most 2 blocks of any one holder, and in every draw one holder is named exactly 2 times by every db index.
All inputs are finite; a program needn't handle non-finite values.
Results may differ from the reference program's by a relative error of at most 0.015.
Values may be sent and summed in bfloat16 or wider, within the bound.
A program may use at most 128 MiB of HBM per device.

```python
import jax
import jax.numpy as jnp
from jax import lax

D = 4096
HEADS = 16
HD = 128
E = 896
EH = 2048
NEIGH = 2
QBLOCK = 64
NBLOCK = 128
DB_DEV = 4
LAYERS = 2
TOKENS = 4096
QB_DB = 8
QBLOCKS = 64
CAP = 2
DB_BLOCKS = 32


def drawn_or_flat(key, array_shape, spread_scale, clip_bound):
    return jnp.clip(jax.random.normal(key, array_shape, jnp.float32), -clip_bound, clip_bound) * spread_scale


def draw_hidden_in(key, part):
    drawn = drawn_or_flat(jax.random.fold_in(key, 1), (TOKENS, D), 1.0, 6.0)
    return drawn.astype(jnp.bfloat16)


def draw_database(key, part):
    drawn = drawn_or_flat(jax.random.fold_in(key, 1), (DB_BLOCKS, NBLOCK, E), 1.0, 6.0)
    return drawn.astype(jnp.bfloat16)


def draw_w_query(key, part):
    drawn = drawn_or_flat(jax.random.fold_in(key, 1), (LAYERS, D, HEADS * HD), D ** (-0.5), 4.0)
    return drawn.astype(jnp.bfloat16)


def draw_w_key(key, part):
    drawn = drawn_or_flat(jax.random.fold_in(key, 1), (LAYERS, E, HEADS * HD), E ** (-0.5), 4.0)
    return drawn.astype(jnp.bfloat16)


def draw_neighbour_ids(key, part):
    holders = QBLOCKS // QB_DB
    request = NEIGH * QB_DB
    slot_count = holders * CAP
    favoured = jax.random.randint(jax.random.fold_in(key, 7), (), 0, holders)

    def one_source(source):
        subkey = jax.random.fold_in(key, source + 100)
        ranking = jax.random.permutation(jax.random.fold_in(subkey, 1), slot_count)
        holder_of = jnp.arange(slot_count) // CAP
        ranking = jnp.where(holder_of == favoured, -1 - jnp.arange(slot_count), ranking)
        ordered = jnp.argsort(ranking, stable=True)[:request]
        ordered = ordered[jax.random.permutation(jax.random.fold_in(subkey, 2), request)]
        owners = ordered // CAP
        within = jax.random.randint(jax.random.fold_in(subkey, 3), (request,), 0, DB_DEV)
        return (owners * DB_DEV + within).astype(jnp.int32)
    id_grid = jax.vmap(one_source)(jnp.arange(holders))
    return id_grid.reshape(QBLOCKS, NEIGH)


def block_levels(stream_key, shape, shards, smallest, top_value):
    gain = 1.0
    for dim, blocks in shards:
        heights = jax.random.uniform(jax.random.fold_in(jax.random.fold_in(stream_key, 6), dim), (blocks,), jnp.float32, smallest / len(shards), top_value / len(shards))
        gain = gain * jnp.repeat(jnp.exp(heights), shape[dim] // blocks).reshape((-1,) + (1,) * (len(shape) - 1 - dim))
    return gain


def gaussian(key, dims, width, most, cuts=(), held_as=jnp.bfloat16):
    level = block_levels(key, dims, cuts, -0.22, 0.18) if cuts else 1.0
    values = jax.random.normal(key, dims, jnp.float32) * width * level
    return jnp.minimum(jnp.maximum(values, -most), most).astype(held_as)


def setup_inputs(seed: int = 0) -> dict:
    arg_keys = jax.random.split(jax.random.key(seed), 12)
    hidden_in = draw_hidden_in(jax.random.fold_in(arg_keys[11], 71), 0)
    database = draw_database(jax.random.fold_in(arg_keys[11], 71), 0)
    neighbour_ids = draw_neighbour_ids(jax.random.fold_in(arg_keys[11], 71), 0)
    enc_gain = jnp.clip(1.0 + 0.18 * jax.random.normal(arg_keys[3], (E,), jnp.float32), 0.1, 1.9)
    enc_up = gaussian(arg_keys[4], (E, EH), E ** -0.5, 0.1875, ((1, 4),))
    enc_down = gaussian(arg_keys[5], (EH, E), EH ** -0.5, 0.125, ((0, 4),))
    dec_gain = jnp.clip(1.0 + 0.18 * jax.random.normal(arg_keys[6], (LAYERS, D), jnp.float32), 0.1, 1.9)
    w_query = draw_w_query(jax.random.fold_in(arg_keys[11], 71), 0)
    w_key = draw_w_key(jax.random.fold_in(arg_keys[11], 71), 0)
    w_value = gaussian(arg_keys[9], (LAYERS, E, HEADS * HD), E ** -0.5, 0.1875, ((0, 2), (2, 2)))
    w_out = gaussian(arg_keys[10], (LAYERS, HEADS * HD, D), (HEADS * HD) ** -0.5, 0.125, ((0, 2), (1, 2)))
    return dict(hidden_in=hidden_in, database=database, neighbour_ids=neighbour_ids, enc_gain=enc_gain, enc_up=enc_up, enc_down=enc_down, dec_gain=dec_gain, w_query=w_query, w_key=w_key, w_value=w_value, w_out=w_out)


def rms_scale(rows_in, gain_vec):
    return rows_in * lax.rsqrt(lax.optimization_barrier(jnp.mean(rows_in * rows_in, axis=-1, keepdims=True)) + 1e-06) * gain_vec

def encode_rows(rows_in, enc_gain, enc_up, enc_down):
    floats = rows_in.astype(jnp.float32)
    normed = rms_scale(floats, enc_gain).astype(jnp.bfloat16)
    inner_act = jax.nn.gelu(jnp.dot(normed, enc_up, preferred_element_type=jnp.float32), approximate=True).astype(jnp.bfloat16)
    return (floats + jnp.dot(inner_act, enc_down, preferred_element_type=jnp.float32)).astype(jnp.bfloat16)

def cross_layer(state_rows, blocks, gain_vec, query_w, key_w, value_w, out_w):
    floats = state_rows.astype(jnp.float32)
    normed = rms_scale(floats, gain_vec).astype(jnp.bfloat16)
    queries = (jnp.dot(normed, query_w, preferred_element_type=jnp.float32) * HD ** (-0.5)).astype(jnp.bfloat16)
    groups = QBLOCKS // QB_DB
    query_groups = queries.reshape(groups, QB_DB, QBLOCK, HEADS * HD)
    block_groups = blocks.reshape(groups, QB_DB, NEIGH * NBLOCK, E)

    def attend(group_pair):
        query_part, block_part = group_pair
        flat_rows = block_part.reshape(-1, E)
        key_rows = jnp.dot(flat_rows, key_w, preferred_element_type=jnp.float32).astype(jnp.bfloat16)
        value_rows = jnp.dot(flat_rows, value_w, preferred_element_type=jnp.float32).astype(jnp.bfloat16)
        query_four = query_part.reshape(QB_DB, QBLOCK, HEADS, HD).astype(jnp.float32)
        key_four = key_rows.reshape(QB_DB, NEIGH * NBLOCK, HEADS, HD).astype(jnp.float32)
        value_four = value_rows.reshape(QB_DB, NEIGH * NBLOCK, HEADS, HD).astype(jnp.float32)
        scores = jnp.einsum('cqhd,ckhd->chqk', query_four, key_four)
        soft_weights = jax.nn.softmax(scores, axis=-1).astype(jnp.bfloat16)
        context = jnp.einsum('chqk,ckhd->cqhd', soft_weights.astype(jnp.float32), value_four)
        return context.astype(jnp.bfloat16).reshape(QB_DB * QBLOCK, HEADS * HD)
    context = lax.map(attend, (query_groups, block_groups)).reshape(TOKENS, HEADS * HD)
    return (floats + jnp.dot(context, out_w, preferred_element_type=jnp.float32)).astype(jnp.bfloat16)

def reference(hidden_in, database, neighbour_ids, enc_gain, enc_up, enc_down, dec_gain, w_query, w_key, w_value, w_out):
    fetched = database[neighbour_ids.reshape(-1)]
    encoded = encode_rows(fetched.reshape(-1, E), enc_gain, enc_up, enc_down)
    encoded = encoded.reshape(QBLOCKS, NEIGH * NBLOCK, E)
    state_rows = hidden_in
    for layer_id in range(LAYERS):
        state_rows = cross_layer(state_rows, encoded, dec_gain[layer_id], w_query[layer_id], w_key[layer_id], w_value[layer_id], w_out[layer_id])
    return state_rows
```

```python
import jax
import jax.numpy as jnp
from jax import lax
from jax.sharding import PartitionSpec as P

HD = 128
E = 896
NEIGH = 2
QBLOCK = 64
NBLOCK = 128
CHUNKS = 2
F32 = jnp.float32
BF16 = jnp.bfloat16


def swap(block, axis):
    return lax.ppermute(block, axis, [(0, 1), (1, 0)])


def rms_scale(rows_in, gain_vec):
    return (
        rows_in * lax.rsqrt(jnp.mean(rows_in * rows_in, axis=-1, keepdims=True) + 1e-06) * gain_vec
    )


def mm(a, b):
    return jnp.dot(a, b, preferred_element_type=F32)


def encode_half(database, enc_gain, enc_up, enc_down):
    section = lax.axis_index("section")
    held = database.shape[0]
    floats = database.reshape(-1, E).astype(F32)
    normed = rms_scale(floats, enc_gain).astype(BF16)
    inner = jax.nn.gelu(mm(normed, enc_up), approximate=True).astype(BF16)
    terms = mm(inner, enc_down).reshape(held, 2, NBLOCK // 2, E)
    mine = lax.dynamic_index_in_dim(terms, section, 1, keepdims=False)
    theirs = lax.dynamic_index_in_dim(terms, 1 - section, 1, keepdims=False)
    mine = mine + swap(theirs, "section")
    mine = mine + swap(mine.astype(BF16), "mp").astype(F32)
    rows = lax.dynamic_index_in_dim(
        database.reshape(held, 2, NBLOCK // 2, E), section, 1, keepdims=False
    )
    return (rows.astype(F32) + mine).astype(BF16)


def fetch(encoded, neighbour_ids):
    section = lax.axis_index("section")
    db_count = lax.axis_size("db")
    db_index = lax.axis_index("db")
    blocks_held = encoded.shape[0]
    request = neighbour_ids.shape[0] // db_count * NEIGH
    capacity = max(2, (request + db_count - 1) // db_count)
    id_table = neighbour_ids.reshape(db_count, request)
    owners = id_table // blocks_held
    within = id_table % blocks_held
    places = jnp.arange(request)
    same_owner = owners[:, :, None] == owners[:, None, :]
    earlier = places[None, :, None] > places[None, None, :]
    rank_in = jnp.sum((same_owner & earlier).astype(jnp.int32), axis=-1)
    slot_ids = jnp.arange(capacity)
    matches = (owners[:, None, :] == db_index) & (rank_in[:, None, :] == slot_ids[None, :, None])
    send_local = jnp.sum(matches.astype(jnp.int32) * within[:, None, :], axis=-1)
    my_owner = lax.dynamic_index_in_dim(owners, db_index, 0, keepdims=False)
    my_rank = lax.dynamic_index_in_dim(rank_in, db_index, 0, keepdims=False)
    slot_pick = (my_owner * capacity + my_rank).reshape(2, request // 2)
    mine = lax.dynamic_index_in_dim(slot_pick, section, 0, keepdims=False)
    theirs = lax.dynamic_index_in_dim(slot_pick, 1 - section, 0, keepdims=False)
    payload = encoded[send_local]
    received = lax.all_to_all(payload, "db", split_axis=0, concat_axis=0, tiled=True)
    received = received.reshape(db_count * capacity, NBLOCK // 2, E)
    return jnp.stack([received[mine], swap(received[theirs], "section")])


def attend(queries, key_rows, value_rows):
    blocks = key_rows.shape[1]
    heads = queries.shape[1] // HD
    q = queries.reshape(blocks, QBLOCK, heads, HD)
    k = key_rows.reshape(2, blocks, NBLOCK, heads, HD)
    v = value_rows.reshape(2, blocks, NBLOCK, heads, HD)
    k = jnp.concatenate([k[0], k[1]], axis=1)
    v = jnp.concatenate([v[0], v[1]], axis=1)
    scores = jnp.einsum("cqhd,ckhd->chqk", q, k, preferred_element_type=F32)
    probs = jax.nn.softmax(scores, axis=-1).astype(BF16)
    context = jnp.einsum("chqk,ckhd->cqhd", probs, v, preferred_element_type=F32)
    return context.astype(BF16).reshape(blocks * QBLOCK, heads * HD)


def body(
    hidden_in,
    database,
    neighbour_ids,
    enc_gain,
    enc_up,
    enc_down,
    dec_gain,
    w_query,
    w_key,
    w_value,
    w_out,
):
    section = lax.axis_index("section")
    mp = lax.axis_index("mp")
    tokens = hidden_in.shape[0] // 2
    blocks = tokens // QBLOCK
    width = hidden_in.shape[1]

    encoded = encode_half(database, enc_gain, enc_up, enc_down)
    entering = lax.dynamic_slice_in_dim(hidden_in, section * tokens, tokens, 0)
    state = lax.all_gather(entering, "mp", axis=1, tiled=True)
    gains = lax.all_gather(dec_gain, "section", axis=0, tiled=True)
    wq = lax.all_gather(w_query, "section", axis=0, tiled=True)
    wk = lax.all_gather(w_key, "section", axis=0, tiled=True)
    wv = lax.all_gather(w_value, "section", axis=0, tiled=True)
    wo = lax.all_gather(w_out, "section", axis=0, tiled=True)

    neighbours = fetch(encoded, neighbour_ids).reshape(-1, E)

    def project(layer):
        k = mm(neighbours, wk[layer]).astype(BF16).reshape(2, blocks, NBLOCK, -1)
        v = mm(neighbours, wv[layer]).astype(BF16).reshape(2, blocks, NBLOCK, -1)
        return k, v

    def query(rows, layer):
        normed = rms_scale(rows.astype(F32), gains[layer]).astype(BF16)
        return (mm(normed, wq[layer]) * HD ** (-0.5)).astype(BF16)

    q0 = query(state, 0)
    k0, v0 = project(0)
    k1, v1 = project(1)
    piece = tokens // CHUNKS
    pb = blocks // CHUNKS
    results = []
    for i in range(CHUNKS):
        span = slice(i * piece, (i + 1) * piece)
        bspan = slice(i * pb, (i + 1) * pb)
        context = attend(q0[span], k0[:, bspan], v0[:, bspan])
        terms = mm(context, wo[0])
        arrived = swap(terms.astype(BF16), "mp")
        mid = (state[span].astype(F32) + terms + arrived.astype(F32)).astype(BF16)
        q1 = query(mid, 1)
        context = attend(q1, k1[:, bspan], v1[:, bspan])
        away = lax.dynamic_slice_in_dim(wo[1], (1 - mp) * width, width, 1)
        home = lax.dynamic_slice_in_dim(wo[1], mp * width, width, 1)
        arrived = swap(mm(context, away).astype(BF16), "mp")
        mine = lax.dynamic_slice_in_dim(mid, mp * width, width, 1)
        results.append(
            (mine.astype(F32) + mm(context, home) + arrived.astype(F32)).astype(BF16)
        )
    return jnp.concatenate(results, axis=0)


def solution(mesh):
    in_specs = (
        P("db", "mp"),
        P("db", None, None),
        P(),
        P(),
        P(None, ("section", "mp")),
        P(("section", "mp"), None),
        P("section", None),
        P("section", None, "mp"),
        P("section", None, "mp"),
        P("section", None, "mp"),
        P("section", "mp", None),
    )
    out_specs = P(("db", "section"), "mp")
    return jax.shard_map(body, mesh=mesh, in_specs=in_specs, out_specs=out_specs, check_vma=False)
```

```python
import functools

import jax
import jax.numpy as jnp
from jax import lax
from jax.experimental import pallas as pl
from jax.experimental.pallas import tpu as pltpu
from jax.sharding import PartitionSpec as P

HD = 128
E = 896
NEIGH = 2
QBLOCK = 64
NBLOCK = 128
CHUNKS = 2
F32 = jnp.float32
BF16 = jnp.bfloat16


def swap(block, axis):
    return lax.ppermute(block, axis, [(0, 1), (1, 0)])


def rms_scale(rows_in, gain_vec):
    return (
        rows_in * lax.rsqrt(jnp.mean(rows_in * rows_in, axis=-1, keepdims=True) + 1e-06) * gain_vec
    )


def mm(a, b):
    return jnp.dot(a, b, preferred_element_type=F32)


def encode_half(database, enc_gain, enc_up, enc_down):
    section = lax.axis_index("section")
    held = database.shape[0]
    floats = database.reshape(-1, E).astype(F32)
    normed = rms_scale(floats, enc_gain).astype(BF16)
    inner = jax.nn.gelu(mm(normed, enc_up), approximate=True).astype(BF16)
    terms = mm(inner, enc_down).reshape(held, 2, NBLOCK // 2, E)
    mine = lax.dynamic_index_in_dim(terms, section, 1, keepdims=False)
    theirs = lax.dynamic_index_in_dim(terms, 1 - section, 1, keepdims=False)
    mine = mine + swap(theirs, "section")
    mine = mine + swap(mine.astype(BF16), "mp").astype(F32)
    rows = lax.dynamic_index_in_dim(
        database.reshape(held, 2, NBLOCK // 2, E), section, 1, keepdims=False
    )
    return (rows.astype(F32) + mine).astype(BF16)


def fetch(encoded, neighbour_ids, fill):
    section = lax.axis_index("section")
    db_count = lax.axis_size("db")
    db_index = lax.axis_index("db")
    blocks_held = encoded.shape[0]
    request = neighbour_ids.shape[0] // db_count * NEIGH
    capacity = max(2, (request + db_count - 1) // db_count)
    id_table = neighbour_ids.reshape(db_count, request)
    owners = id_table // blocks_held
    within = id_table % blocks_held
    places = jnp.arange(request)
    same_owner = owners[:, :, None] == owners[:, None, :]
    earlier = places[None, :, None] > places[None, None, :]
    rank_in = jnp.sum((same_owner & earlier).astype(jnp.int32), axis=-1)
    slot_ids = jnp.arange(capacity)
    matches = (owners[:, None, :] == db_index) & (rank_in[:, None, :] == slot_ids[None, :, None])
    send_local = jnp.sum(matches.astype(jnp.int32) * within[:, None, :], axis=-1)
    my_owner = lax.dynamic_index_in_dim(owners, db_index, 0, keepdims=False)
    my_rank = lax.dynamic_index_in_dim(rank_in, db_index, 0, keepdims=False)
    slot_pick = (my_owner * capacity + my_rank).reshape(2, request // 2)
    mine = lax.dynamic_index_in_dim(slot_pick, section, 0, keepdims=False)
    theirs = lax.dynamic_index_in_dim(slot_pick, 1 - section, 0, keepdims=False)
    payload = encoded[send_local]
    received = lax.all_to_all(payload, "db", split_axis=0, concat_axis=0, tiled=True)
    received, fill = lax.optimization_barrier((received, fill))
    received = received.reshape(db_count * capacity, NBLOCK // 2, E)
    moved = swap(received[theirs], "section")
    return received[mine].reshape(-1, E), moved.reshape(-1, E), fill


def kv_kernel(rows, wk, wv, k, v):
    k[...] = mm(rows[...], wk[0]).astype(BF16)
    v[...] = mm(rows[...], wv[0]).astype(BF16)


def keys_values(rows, wk, wv, layer):
    count, out = rows.shape[0], wk.shape[2]
    tile = 256
    weight = pl.BlockSpec((1, E, out), lambda i: (layer, 0, 0))
    made = pl.BlockSpec((tile, out), lambda i: (i, 0))
    k, v = pl.pallas_call(
        kv_kernel,
        grid=(count // tile,),
        in_specs=[pl.BlockSpec((tile, E), lambda i: (i, 0)), weight, weight],
        out_specs=[made, made],
        out_shape=[jax.ShapeDtypeStruct((count, out), BF16)] * 2,
        compiler_params=pltpu.CompilerParams(vmem_limit_bytes=40 << 20),
        cost_estimate=pl.CostEstimate(
            flops=4 * count * E * out,
            bytes_accessed=4 * E * out + 2 * count * E + 4 * count * out,
            transcendentals=0,
        ),
    )(rows, wk, wv)
    shape = (count // NBLOCK, NBLOCK, out)
    return k.reshape(shape), v.reshape(shape)


def attend_heads(q, ks, vs, block, heads):
    made = []
    for h in range(heads):
        cols = slice(h * HD, (h + 1) * HD)
        k = jnp.concatenate([ref[block, :, cols] for ref in ks], axis=0)
        v = jnp.concatenate([ref[block, :, cols] for ref in vs], axis=0)
        scores = lax.dot_general(
            q[:, cols], k, (((1,), (1,)), ((), ())), preferred_element_type=F32
        )
        e = jnp.exp(scores - jnp.max(scores, axis=-1, keepdims=True))
        probs = (e / jnp.sum(e, axis=-1, keepdims=True)).astype(BF16)
        made.append(mm(probs, v).astype(BF16))
    return jnp.concatenate(made, axis=1)


def first_kernel(blocks, heads, q, ka, kb, va, vb, wo, state, send, base, ctx):
    @pl.when(pl.program_id(0) == 0)
    def _():
        for b in range(blocks):
            rows = slice(b * QBLOCK, (b + 1) * QBLOCK)
            ctx[rows, :] = attend_heads(q[rows, :], (ka, kb), (va, vb), b, heads)

    terms = mm(ctx[...], wo[0])
    send[...] = terms.astype(BF16)
    base[...] = state[...].astype(F32) + terms


def first_layer(q, kv, wo, state, part, piece):
    ka, kb, va, vb = kv
    blocks = piece // QBLOCK
    inner, width = wo.shape[1], wo.shape[2]
    tile = 512
    around = pl.BlockSpec((blocks, NBLOCK, inner), lambda j: (part, 0, 0))
    made = pl.BlockSpec((piece, tile), lambda j: (0, j))
    return pl.pallas_call(
        functools.partial(first_kernel, blocks, inner // HD),
        grid=(width // tile,),
        in_specs=[
            pl.BlockSpec((piece, inner), lambda j: (part, 0)),
            around,
            around,
            around,
            around,
            pl.BlockSpec((1, inner, tile), lambda j: (0, 0, j)),
            pl.BlockSpec((piece, tile), lambda j: (part, j)),
        ],
        out_specs=[made, made],
        out_shape=[
            jax.ShapeDtypeStruct((piece, width), BF16),
            jax.ShapeDtypeStruct((piece, width), F32),
        ],
        scratch_shapes=[pltpu.VMEM((piece, inner), BF16)],
        compiler_params=pltpu.CompilerParams(vmem_limit_bytes=40 << 20),
        cost_estimate=pl.CostEstimate(
            flops=2 * piece * inner * (width + 512),
            bytes_accessed=2 * inner * width + 8 * piece * width,
            transcendentals=piece * 256 * inner // HD,
        ),
    )(q, ka, kb, va, vb, wo, state)


def second_kernel(
    blocks, q_steps, away, mp, base, arrived, gain, wq, ka, kb, va, vb, wo, send, home, normed, mid, ctx
):
    j = pl.program_id(0)
    q_tile = wq.shape[2]
    tile = wo.shape[2]

    @pl.when(j == 0)
    def _():
        whole = (base[...] + arrived[...].astype(F32)).astype(BF16)
        mid[...] = whole
        normed[...] = rms_scale(whole.astype(F32), gain[...]).astype(BF16)

    @pl.when(j < q_steps)
    def _():
        q = (mm(normed[...], wq[0]) * HD ** (-0.5)).astype(BF16)
        cols = pl.ds(pl.multiple_of(j * q_tile, q_tile), q_tile)
        for b in range(blocks):
            rows = slice(b * QBLOCK, (b + 1) * QBLOCK)
            ctx[rows, cols] = attend_heads(q[rows, :], (ka, kb), (va, vb), b, q_tile // HD)

    @pl.when((j >= q_steps) & (j < q_steps + away))
    def _():
        send[...] = mm(ctx[...], wo[0]).astype(BF16)

    @pl.when(j >= q_steps + away)
    def _():
        start = pl.multiple_of((mp[0] * away + j - q_steps - away) * tile, tile)
        home[...] = mid[:, pl.ds(start, tile)].astype(F32) + mm(ctx[...], wo[0])


def second_layer(mp, base, arrived, gain, wq, kv, wo, part):
    ka, kb, va, vb = kv
    piece, width = base.shape
    blocks = piece // QBLOCK
    inner = wo.shape[1]
    q_tile, tile = 256, 512
    q_steps = inner // q_tile
    away = width // 2 // tile
    around = pl.BlockSpec(
        (blocks, NBLOCK, q_tile), lambda j, m: (part, 0, jnp.minimum(j, q_steps - 1))
    )
    whole = pl.BlockSpec((piece, width), lambda j, m: (0, 0))

    def out_column(j, m):
        t = jnp.maximum(j - q_steps, 0)
        return (1, 0, jnp.where(t < away, (1 - m[0]) * away + t, m[0] * away + t - away))

    return pl.pallas_call(
        functools.partial(second_kernel, blocks, q_steps, away),
        grid_spec=pltpu.PrefetchScalarGridSpec(
            num_scalar_prefetch=1,
            grid=(q_steps + 2 * away,),
            in_specs=[
                whole,
                whole,
                pl.BlockSpec((1, width), lambda j, m: (0, 0)),
                pl.BlockSpec(
                    (1, width, q_tile), lambda j, m: (1, 0, jnp.minimum(j, q_steps - 1))
                ),
                around,
                around,
                around,
                around,
                pl.BlockSpec((1, inner, tile), out_column),
            ],
            out_specs=[
                pl.BlockSpec((piece, tile), lambda j, m: (0, jnp.clip(j - q_steps, 0, away - 1))),
                pl.BlockSpec(
                    (piece, tile), lambda j, m: (0, jnp.clip(j - q_steps - away, 0, away - 1))
                ),
            ],
            scratch_shapes=[
                pltpu.VMEM((piece, width), BF16),
                pltpu.VMEM((piece, width), BF16),
                pltpu.VMEM((piece, inner), BF16),
            ],
        ),
        out_shape=[
            jax.ShapeDtypeStruct((piece, width // 2), BF16),
            jax.ShapeDtypeStruct((piece, width // 2), F32),
        ],
        compiler_params=pltpu.CompilerParams(vmem_limit_bytes=40 << 20),
        cost_estimate=pl.CostEstimate(
            flops=4 * piece * inner * width,
            bytes_accessed=4 * inner * width + 12 * piece * width,
            transcendentals=piece * 256 * inner // HD,
        ),
    )(mp, base, arrived, gain, wq, ka, kb, va, vb, wo)


def body(
    hidden_in,
    database,
    neighbour_ids,
    enc_gain,
    enc_up,
    enc_down,
    dec_gain,
    w_query,
    w_key,
    w_value,
    w_out,
):
    section = lax.axis_index("section")
    mp = lax.axis_index("mp")
    tokens = hidden_in.shape[0] // 2

    encoded = encode_half(database, enc_gain, enc_up, enc_down)
    entering = lax.dynamic_slice_in_dim(hidden_in, section * tokens, tokens, 0)
    encoded, entering = lax.optimization_barrier((encoded, entering))
    other = swap(entering, "mp")
    state = jnp.where(
        mp == 0,
        jnp.concatenate([entering, other], axis=1),
        jnp.concatenate([other, entering], axis=1),
    )
    gains = lax.all_gather(dec_gain, "section", axis=0, tiled=True)
    wq = lax.all_gather(w_query, "section", axis=0, tiled=True)
    wk = lax.all_gather(w_key, "section", axis=0, tiled=True)
    wv = lax.all_gather(w_value, "section", axis=0, tiled=True)
    wo = lax.all_gather(w_out, "section", axis=0, tiled=True)

    normed = rms_scale(state.astype(F32), gains[0]).astype(BF16)
    q0 = (mm(normed, wq[0]) * HD ** (-0.5)).astype(BF16)
    rows_a, rows_b, q0 = fetch(encoded, neighbour_ids, q0)

    def around(layer):
        ka, va = keys_values(rows_a, wk, wv, layer)
        kb, vb = keys_values(rows_b, wk, wv, layer)
        return ka, kb, va, vb

    kv0 = around(0)
    kv1 = around(1)
    piece = tokens // CHUNKS
    mp_scalar = mp.astype(jnp.int32).reshape(1)
    sent = [first_layer(q0, kv0, wo, state, i, piece) for i in range(CHUNKS)]
    arrived = [swap(send, "mp") for send, _ in sent]
    results = []
    for i in range(CHUNKS):
        send, home = second_layer(mp_scalar, sent[i][1], arrived[i], gains[1:2], wq, kv1, wo, i)
        results.append((home + swap(send, "mp").astype(F32)).astype(BF16))
    return jnp.concatenate(results, axis=0)


def solution(mesh):
    in_specs = (
        P("db", "mp"),
        P("db", None, None),
        P(),
        P(),
        P(None, ("section", "mp")),
        P(("section", "mp"), None),
        P("section", None),
        P("section", None, "mp"),
        P("section", None, "mp"),
        P("section", None, "mp"),
        P("section", "mp", None),
    )
    out_specs = P(("db", "section"), "mp")
    return jax.shard_map(body, mesh=mesh, in_specs=in_specs, out_specs=out_specs, check_vma=False)
```

```python
import functools

import jax
import jax.numpy as jnp
from jax import lax
from jax.experimental import pallas as pl
from jax.experimental.pallas import tpu as pltpu
from jax.sharding import PartitionSpec as P

HD = 128
E = 896
NEIGH = 2
QBLOCK = 64
NBLOCK = 128
CHUNKS = 2
VMEM_BYTES = 62 << 20
F32 = jnp.float32
BF16 = jnp.bfloat16


def swap(block, axis):
    return lax.ppermute(block, axis, [(0, 1), (1, 0)])


def rms_scale(rows_in, gain_vec):
    return (
        rows_in * lax.rsqrt(jnp.mean(rows_in * rows_in, axis=-1, keepdims=True) + 1e-06) * gain_vec
    )


def mm(a, b):
    return jnp.dot(a, b, preferred_element_type=F32)


def encode_half(database, enc_gain, enc_up, enc_down, first):
    section = lax.axis_index("section")
    held = database.shape[0]
    floats = database.reshape(-1, E).astype(F32)
    normed = rms_scale(floats, enc_gain).astype(BF16)
    inner = jax.nn.gelu(mm(normed, enc_up), approximate=True).astype(BF16)
    terms = mm(inner, enc_down).reshape(held, 2, NBLOCK // 2, E)
    mine = lax.dynamic_index_in_dim(terms, section, 1, keepdims=False)
    theirs = lax.dynamic_index_in_dim(terms, 1 - section, 1, keepdims=False)
    mine = mine + swap(theirs, "section")
    mine, first = lax.optimization_barrier((mine, first))
    mine = mine + swap(mine.astype(BF16), "mp").astype(F32)
    rows = lax.dynamic_index_in_dim(
        database.reshape(held, 2, NBLOCK // 2, E), section, 1, keepdims=False
    )
    return (rows.astype(F32) + mine).astype(BF16), first


def fetch(encoded, neighbour_ids, fill):
    section = lax.axis_index("section")
    db_count = lax.axis_size("db")
    db_index = lax.axis_index("db")
    blocks_held = encoded.shape[0]
    request = neighbour_ids.shape[0] // db_count * NEIGH
    capacity = max(2, (request + db_count - 1) // db_count)
    id_table = neighbour_ids.reshape(db_count, request)
    owners = id_table // blocks_held
    within = id_table % blocks_held
    places = jnp.arange(request)
    same_owner = owners[:, :, None] == owners[:, None, :]
    earlier = places[None, :, None] > places[None, None, :]
    rank_in = jnp.sum((same_owner & earlier).astype(jnp.int32), axis=-1)
    slot_ids = jnp.arange(capacity)
    matches = (owners[:, None, :] == db_index) & (rank_in[:, None, :] == slot_ids[None, :, None])
    send_local = jnp.sum(matches.astype(jnp.int32) * within[:, None, :], axis=-1)
    my_owner = lax.dynamic_index_in_dim(owners, db_index, 0, keepdims=False)
    my_rank = lax.dynamic_index_in_dim(rank_in, db_index, 0, keepdims=False)
    slot_pick = (my_owner * capacity + my_rank).reshape(2, request // 2)
    mine = lax.dynamic_index_in_dim(slot_pick, section, 0, keepdims=False)
    theirs = lax.dynamic_index_in_dim(slot_pick, 1 - section, 0, keepdims=False)
    payload = encoded[send_local]
    received = lax.all_to_all(payload, "db", split_axis=0, concat_axis=0, tiled=True)
    received, fill = lax.optimization_barrier((received, fill))
    received = received.reshape(db_count * capacity, NBLOCK // 2, E)
    moved = swap(received[theirs], "section")
    return received[mine].reshape(-1, E), moved.reshape(-1, E), fill


def kv_kernel(rows, wk, wv, k, v):
    k[...] = mm(rows[...], wk[0]).astype(BF16)
    v[...] = mm(rows[...], wv[0]).astype(BF16)


def keys_values(rows, wk, wv, layer):
    count, out = rows.shape[0], wk.shape[2]
    tile = 256
    weight = pl.BlockSpec((1, E, out), lambda i: (layer, 0, 0))
    made = pl.BlockSpec((tile, out), lambda i: (i, 0))
    k, v = pl.pallas_call(
        kv_kernel,
        grid=(count // tile,),
        in_specs=[pl.BlockSpec((tile, E), lambda i: (i, 0)), weight, weight],
        out_specs=[made, made],
        out_shape=[jax.ShapeDtypeStruct((count, out), BF16)] * 2,
        compiler_params=pltpu.CompilerParams(vmem_limit_bytes=VMEM_BYTES),
        cost_estimate=pl.CostEstimate(
            flops=4 * count * E * out,
            bytes_accessed=4 * E * out + 2 * count * E + 4 * count * out,
            transcendentals=0,
        ),
    )(rows, wk, wv)
    shape = (count // NBLOCK, NBLOCK, out)
    return k.reshape(shape), v.reshape(shape)


def attend_heads(q, ks, vs, blocks, heads):
    places = [(b, slice(h * HD, (h + 1) * HD)) for b in range(blocks) for h in range(heads)]
    scores = []
    for b, cols in places:
        k = jnp.concatenate([ref[b, :, cols] for ref in ks], axis=0)
        rows = slice(b * QBLOCK, (b + 1) * QBLOCK)
        scores.append(
            lax.dot_general(
                q[rows, cols], k, (((1,), (1,)), ((), ())), preferred_element_type=F32
            )
        )
    scores = jnp.concatenate(scores, axis=0)
    e = jnp.exp(scores - jnp.max(scores, axis=-1, keepdims=True))
    probs = (e / jnp.sum(e, axis=-1, keepdims=True)).astype(BF16)
    made = []
    for i, (b, cols) in enumerate(places):
        v = jnp.concatenate([ref[b, :, cols] for ref in vs], axis=0)
        made.append(mm(probs[i * QBLOCK : (i + 1) * QBLOCK], v).astype(BF16))
    rows = [jnp.concatenate(made[b * heads : (b + 1) * heads], axis=1) for b in range(blocks)]
    return jnp.concatenate(rows, axis=0)


def first_kernel(blocks, heads, q, ka, kb, va, vb, wo, state, send, base, ctx):
    @pl.when(pl.program_id(0) == 0)
    def _():
        ctx[...] = attend_heads(q[...], (ka, kb), (va, vb), blocks, heads)

    terms = mm(ctx[...], wo[0])
    send[...] = terms.astype(BF16)
    base[...] = state[...].astype(F32) + terms


def first_layer(q, kv, wo, state, part, piece):
    ka, kb, va, vb = kv
    blocks = piece // QBLOCK
    inner, width = wo.shape[1], wo.shape[2]
    tile = 512
    around = pl.BlockSpec((blocks, NBLOCK, inner), lambda j: (part, 0, 0))
    made = pl.BlockSpec((piece, tile), lambda j: (0, j))
    return pl.pallas_call(
        functools.partial(first_kernel, blocks, inner // HD),
        grid=(width // tile,),
        in_specs=[
            pl.BlockSpec((piece, inner), lambda j: (part, 0)),
            around,
            around,
            around,
            around,
            pl.BlockSpec((1, inner, tile), lambda j: (0, 0, j)),
            pl.BlockSpec((piece, tile), lambda j: (part, j)),
        ],
        out_specs=[made, made],
        out_shape=[
            jax.ShapeDtypeStruct((piece, width), BF16),
            jax.ShapeDtypeStruct((piece, width), F32),
        ],
        scratch_shapes=[pltpu.VMEM((piece, inner), BF16)],
        compiler_params=pltpu.CompilerParams(vmem_limit_bytes=VMEM_BYTES),
        cost_estimate=pl.CostEstimate(
            flops=2 * piece * inner * (width + 512),
            bytes_accessed=2 * inner * width + 8 * piece * width,
            transcendentals=piece * 256 * inner // HD,
        ),
    )(q, ka, kb, va, vb, wo, state)


def second_kernel(
    blocks, q_steps, away, mp, base, arrived, gain, wq, ka, kb, va, vb, wo, send, home, normed, mid, ctx
):
    j = pl.program_id(0)
    q_tile = wq.shape[2]
    tile = wo.shape[2]

    @pl.when(j == 0)
    def _():
        whole = (base[...] + arrived[...].astype(F32)).astype(BF16)
        mid[...] = whole
        normed[...] = rms_scale(whole.astype(F32), gain[...]).astype(BF16)

    @pl.when(j < q_steps)
    def _():
        q = (mm(normed[...], wq[0]) * HD ** (-0.5)).astype(BF16)
        cols = pl.ds(pl.multiple_of(j * q_tile, q_tile), q_tile)
        ctx[:, cols] = attend_heads(q, (ka, kb), (va, vb), blocks, q_tile // HD)

    @pl.when((j >= q_steps) & (j < q_steps + away))
    def _():
        send[...] = mm(ctx[...], wo[0]).astype(BF16)

    @pl.when(j >= q_steps + away)
    def _():
        start = pl.multiple_of((mp[0] * away + j - q_steps - away) * tile, tile)
        home[...] = mid[:, pl.ds(start, tile)].astype(F32) + mm(ctx[...], wo[0])


def second_layer(mp, base, arrived, gain, wq, kv, wo, part):
    ka, kb, va, vb = kv
    piece, width = base.shape
    blocks = piece // QBLOCK
    inner = wo.shape[1]
    q_tile, tile = 256, 512
    q_steps = inner // q_tile
    away = width // 2 // tile
    around = pl.BlockSpec(
        (blocks, NBLOCK, q_tile), lambda j, m: (part, 0, jnp.minimum(j, q_steps - 1))
    )
    whole = pl.BlockSpec((piece, width), lambda j, m: (0, 0))

    def out_column(j, m):
        t = jnp.maximum(j - q_steps, 0)
        return (1, 0, jnp.where(t < away, (1 - m[0]) * away + t, m[0] * away + t - away))

    return pl.pallas_call(
        functools.partial(second_kernel, blocks, q_steps, away),
        grid_spec=pltpu.PrefetchScalarGridSpec(
            num_scalar_prefetch=1,
            grid=(q_steps + 2 * away,),
            in_specs=[
                whole,
                whole,
                pl.BlockSpec((1, width), lambda j, m: (0, 0)),
                pl.BlockSpec(
                    (1, width, q_tile), lambda j, m: (1, 0, jnp.minimum(j, q_steps - 1))
                ),
                around,
                around,
                around,
                around,
                pl.BlockSpec((1, inner, tile), out_column),
            ],
            out_specs=[
                pl.BlockSpec((piece, tile), lambda j, m: (0, jnp.clip(j - q_steps, 0, away - 1))),
                pl.BlockSpec(
                    (piece, tile), lambda j, m: (0, jnp.clip(j - q_steps - away, 0, away - 1))
                ),
            ],
            scratch_shapes=[
                pltpu.VMEM((piece, width), BF16),
                pltpu.VMEM((piece, width), BF16),
                pltpu.VMEM((piece, inner), BF16),
            ],
        ),
        out_shape=[
            jax.ShapeDtypeStruct((piece, width // 2), BF16),
            jax.ShapeDtypeStruct((piece, width // 2), F32),
        ],
        compiler_params=pltpu.CompilerParams(vmem_limit_bytes=VMEM_BYTES),
        cost_estimate=pl.CostEstimate(
            flops=4 * piece * inner * width,
            bytes_accessed=4 * inner * width + 12 * piece * width,
            transcendentals=piece * 256 * inner // HD,
        ),
    )(mp, base, arrived, gain, wq, ka, kb, va, vb, wo)


def body(
    hidden_in,
    database,
    neighbour_ids,
    enc_gain,
    enc_up,
    enc_down,
    dec_gain,
    w_query,
    w_key,
    w_value,
    w_out,
):
    section = lax.axis_index("section")
    mp = lax.axis_index("mp")
    tokens = hidden_in.shape[0] // 2

    entering = lax.dynamic_slice_in_dim(hidden_in, section * tokens, tokens, 0)
    other = swap(entering, "mp")
    encoded, other = encode_half(database, enc_gain, enc_up, enc_down, other)
    state = jnp.where(
        mp == 0,
        jnp.concatenate([entering, other], axis=1),
        jnp.concatenate([other, entering], axis=1),
    )
    gains = lax.all_gather(dec_gain, "section", axis=0, tiled=True)
    wq = lax.all_gather(w_query, "section", axis=0, tiled=True)
    wk = lax.all_gather(w_key, "section", axis=0, tiled=True)
    wv = lax.all_gather(w_value, "section", axis=0, tiled=True)
    wo = lax.all_gather(w_out, "section", axis=0, tiled=True)

    normed = rms_scale(state.astype(F32), gains[0]).astype(BF16)
    q0 = (mm(normed, wq[0]) * HD ** (-0.5)).astype(BF16)
    rows_a, rows_b, q0 = fetch(encoded, neighbour_ids, q0)

    def around(layer):
        ka, va = keys_values(rows_a, wk, wv, layer)
        kb, vb = keys_values(rows_b, wk, wv, layer)
        return ka, kb, va, vb

    kv0 = around(0)
    kv1 = around(1)
    piece = tokens // CHUNKS
    mp_scalar = mp.astype(jnp.int32).reshape(1)
    sent = [first_layer(q0, kv0, wo, state, i, piece) for i in range(CHUNKS)]
    arrived = [swap(send, "mp") for send, _ in sent]
    results = []
    for i in range(CHUNKS):
        send, home = second_layer(mp_scalar, sent[i][1], arrived[i], gains[1:2], wq, kv1, wo, i)
        results.append((home + swap(send, "mp").astype(F32)).astype(BF16))
    return jnp.concatenate(results, axis=0)


def solution(mesh):
    in_specs = (
        P("db", "mp"),
        P("db", None, None),
        P(),
        P(),
        P(None, ("section", "mp")),
        P(("section", "mp"), None),
        P("section", None),
        P("section", None, "mp"),
        P("section", None, "mp"),
        P("section", None, "mp"),
        P("section", "mp", None),
    )
    out_specs = P(("db", "section"), "mp")
    return jax.shard_map(body, mesh=mesh, in_specs=in_specs, out_specs=out_specs, check_vma=False)
```

```python
import functools

import jax
import jax.numpy as jnp
from jax import lax
from jax.experimental import pallas as pl
from jax.experimental.pallas import tpu as pltpu
from jax.sharding import PartitionSpec as P

HD = 128
E = 896
NEIGH = 2
QBLOCK = 64
NBLOCK = 128
CHUNKS = 2
VMEM_BYTES = 62 << 20
F32 = jnp.float32
BF16 = jnp.bfloat16


def swap(block, axis):
    return lax.ppermute(block, axis, [(0, 1), (1, 0)])


def rms_scale(rows_in, gain_vec):
    return (
        rows_in * lax.rsqrt(jnp.mean(rows_in * rows_in, axis=-1, keepdims=True) + 1e-06) * gain_vec
    )


def mm(a, b):
    return jnp.dot(a, b, preferred_element_type=F32)


def encode_quarter(database, enc_gain, enc_up, enc_down):
    section = lax.axis_index("section")
    mp = lax.axis_index("mp")
    held = database.shape[0]
    floats = database.reshape(-1, E).astype(F32)
    normed = rms_scale(floats, enc_gain).astype(BF16)
    inner = jax.nn.gelu(mm(normed, enc_up), approximate=True).astype(BF16)
    terms = mm(inner, enc_down).reshape(held, 2, NBLOCK // 2, E)
    mine = lax.dynamic_index_in_dim(terms, section, 1, keepdims=False)
    theirs = lax.dynamic_index_in_dim(terms, 1 - section, 1, keepdims=False)
    mine = (mine + swap(theirs, "section")).reshape(held, 2, NBLOCK // 4, E)
    away = lax.dynamic_index_in_dim(mine, 1 - mp, 1, keepdims=False)
    home = lax.dynamic_index_in_dim(mine, mp, 1, keepdims=False)
    home = home + swap(away.astype(BF16), "mp").astype(F32)
    rows = lax.dynamic_index_in_dim(
        database.reshape(held, 4, NBLOCK // 4, E), section * 2 + mp, 1, keepdims=False
    )
    return (rows.astype(F32) + home).astype(BF16)


def fetch(encoded, neighbour_ids, fill):
    section = lax.axis_index("section")
    db_count = lax.axis_size("db")
    db_index = lax.axis_index("db")
    blocks_held = encoded.shape[0]
    request = neighbour_ids.shape[0] // db_count * NEIGH
    capacity = max(2, (request + db_count - 1) // db_count)
    id_table = neighbour_ids.reshape(db_count, request)
    owners = id_table // blocks_held
    within = id_table % blocks_held
    places = jnp.arange(request)
    same_owner = owners[:, :, None] == owners[:, None, :]
    earlier = places[None, :, None] > places[None, None, :]
    rank_in = jnp.sum((same_owner & earlier).astype(jnp.int32), axis=-1)
    slot_ids = jnp.arange(capacity)
    matches = (owners[:, None, :] == db_index) & (rank_in[:, None, :] == slot_ids[None, :, None])
    send_local = jnp.sum(matches.astype(jnp.int32) * within[:, None, :], axis=-1)
    my_owner = lax.dynamic_index_in_dim(owners, db_index, 0, keepdims=False)
    my_rank = lax.dynamic_index_in_dim(rank_in, db_index, 0, keepdims=False)
    slot_pick = (my_owner * capacity + my_rank).reshape(2, request // 2)
    mine = lax.dynamic_index_in_dim(slot_pick, section, 0, keepdims=False)
    theirs = lax.dynamic_index_in_dim(slot_pick, 1 - section, 0, keepdims=False)
    payload = encoded[send_local]
    received = lax.all_to_all(payload, "db", split_axis=0, concat_axis=0, tiled=True)
    received, fill = lax.optimization_barrier((received, fill))
    received = received.reshape(db_count * capacity, NBLOCK // 4, E)
    moved = swap(received[theirs], "section")
    groups = request // 2 // NEIGH
    near = jnp.concatenate(
        [received[mine].reshape(groups, -1, E), moved.reshape(groups, -1, E)], axis=1
    ).reshape(-1, E)
    return near, swap(near, "mp"), fill


def kv_kernel(rows, wk, wv, k, v):
    k[...] = mm(rows[...], wk[0]).astype(BF16)
    v[...] = mm(rows[...], wv[0]).astype(BF16)


def keys_values(rows, wk, wv, layer):
    count, out = rows.shape[0], wk.shape[2]
    tile = 256
    weight = pl.BlockSpec((1, E, out), lambda i: (layer, 0, 0))
    made = pl.BlockSpec((tile, out), lambda i: (i, 0))
    k, v = pl.pallas_call(
        kv_kernel,
        grid=(count // tile,),
        in_specs=[pl.BlockSpec((tile, E), lambda i: (i, 0)), weight, weight],
        out_specs=[made, made],
        out_shape=[jax.ShapeDtypeStruct((count, out), BF16)] * 2,
        compiler_params=pltpu.CompilerParams(vmem_limit_bytes=VMEM_BYTES),
        cost_estimate=pl.CostEstimate(
            flops=4 * count * E * out,
            bytes_accessed=4 * E * out + 2 * count * E + 4 * count * out,
            transcendentals=0,
        ),
    )(rows, wk, wv)
    shape = (count // NBLOCK, NBLOCK, out)
    return k.reshape(shape), v.reshape(shape)


def attend_heads(q, ks, vs, blocks, heads):
    places = [(b, slice(h * HD, (h + 1) * HD)) for b in range(blocks) for h in range(heads)]
    scores = []
    for b, cols in places:
        k = jnp.concatenate([ref[b, :, cols] for ref in ks], axis=0)
        rows = slice(b * QBLOCK, (b + 1) * QBLOCK)
        scores.append(
            lax.dot_general(
                q[rows, cols], k, (((1,), (1,)), ((), ())), preferred_element_type=F32
            )
        )
    scores = jnp.concatenate(scores, axis=0)
    e = jnp.exp(scores - jnp.max(scores, axis=-1, keepdims=True))
    probs = (e / jnp.sum(e, axis=-1, keepdims=True)).astype(BF16)
    made = []
    for i, (b, cols) in enumerate(places):
        v = jnp.concatenate([ref[b, :, cols] for ref in vs], axis=0)
        made.append(mm(probs[i * QBLOCK : (i + 1) * QBLOCK], v).astype(BF16))
    rows = [jnp.concatenate(made[b * heads : (b + 1) * heads], axis=1) for b in range(blocks)]
    return jnp.concatenate(rows, axis=0)


def first_kernel(blocks, heads, q, ka, kb, va, vb, wo, state, send, base, ctx):
    @pl.when(pl.program_id(0) == 0)
    def _():
        ctx[...] = attend_heads(q[...], (ka, kb), (va, vb), blocks, heads)

    terms = mm(ctx[...], wo[0])
    send[...] = terms.astype(BF16)
    base[...] = state[...].astype(F32) + terms


def first_layer(q, kv, wo, state, part, piece):
    ka, kb, va, vb = kv
    blocks = piece // QBLOCK
    inner, width = wo.shape[1], wo.shape[2]
    tile = 1024
    around = pl.BlockSpec((blocks, NBLOCK, inner), lambda j: (part, 0, 0))
    made = pl.BlockSpec((piece, tile), lambda j: (0, j))
    return pl.pallas_call(
        functools.partial(first_kernel, blocks, inner // HD),
        grid=(width // tile,),
        in_specs=[
            pl.BlockSpec((piece, inner), lambda j: (part, 0)),
            around,
            around,
            around,
            around,
            pl.BlockSpec((1, inner, tile), lambda j: (0, 0, j)),
            pl.BlockSpec((piece, tile), lambda j: (part, j)),
        ],
        out_specs=[made, made],
        out_shape=[
            jax.ShapeDtypeStruct((piece, width), BF16),
            jax.ShapeDtypeStruct((piece, width), F32),
        ],
        scratch_shapes=[pltpu.VMEM((piece, inner), BF16)],
        compiler_params=pltpu.CompilerParams(vmem_limit_bytes=VMEM_BYTES),
        cost_estimate=pl.CostEstimate(
            flops=2 * piece * inner * (width + 512),
            bytes_accessed=2 * inner * width + 8 * piece * width,
            transcendentals=piece * 256 * inner // HD,
        ),
    )(q, ka, kb, va, vb, wo, state)


def second_kernel(
    blocks, q_steps, away, mp, base, arrived, gain, wq, ka, kb, va, vb, wo, send, home, normed, mid, ctx
):
    j = pl.program_id(0)
    q_tile = wq.shape[2]
    tile = wo.shape[2]

    @pl.when(j == 0)
    def _():
        whole = (base[...] + arrived[...].astype(F32)).astype(BF16)
        mid[...] = whole
        normed[...] = rms_scale(whole.astype(F32), gain[...]).astype(BF16)

    @pl.when(j < q_steps)
    def _():
        q = (mm(normed[...], wq[0]) * HD ** (-0.5)).astype(BF16)
        cols = pl.ds(pl.multiple_of(j * q_tile, q_tile), q_tile)
        ctx[:, cols] = attend_heads(q, (ka, kb), (va, vb), blocks, q_tile // HD)

    @pl.when((j >= q_steps) & (j < q_steps + away))
    def _():
        send[...] = mm(ctx[...], wo[0]).astype(BF16)

    @pl.when(j >= q_steps + away)
    def _():
        start = pl.multiple_of((mp[0] * away + j - q_steps - away) * tile, tile)
        home[...] = mid[:, pl.ds(start, tile)].astype(F32) + mm(ctx[...], wo[0])


def second_layer(mp, base, arrived, gain, wq, kv, wo, part):
    ka, kb, va, vb = kv
    piece, width = base.shape
    blocks = piece // QBLOCK
    inner = wo.shape[1]
    q_tile, tile = 256, 1024
    q_steps = inner // q_tile
    away = width // 2 // tile
    around = pl.BlockSpec(
        (blocks, NBLOCK, q_tile), lambda j, m: (part, 0, jnp.minimum(j, q_steps - 1))
    )
    whole = pl.BlockSpec((piece, width), lambda j, m: (0, 0))

    def out_column(j, m):
        t = jnp.maximum(j - q_steps, 0)
        return (1, 0, jnp.where(t < away, (1 - m[0]) * away + t, m[0] * away + t - away))

    return pl.pallas_call(
        functools.partial(second_kernel, blocks, q_steps, away),
        grid_spec=pltpu.PrefetchScalarGridSpec(
            num_scalar_prefetch=1,
            grid=(q_steps + 2 * away,),
            in_specs=[
                whole,
                whole,
                pl.BlockSpec((1, width), lambda j, m: (0, 0)),
                pl.BlockSpec(
                    (1, width, q_tile), lambda j, m: (1, 0, jnp.minimum(j, q_steps - 1))
                ),
                around,
                around,
                around,
                around,
                pl.BlockSpec((1, inner, tile), out_column),
            ],
            out_specs=[
                pl.BlockSpec((piece, tile), lambda j, m: (0, jnp.clip(j - q_steps, 0, away - 1))),
                pl.BlockSpec(
                    (piece, tile), lambda j, m: (0, jnp.clip(j - q_steps - away, 0, away - 1))
                ),
            ],
            scratch_shapes=[
                pltpu.VMEM((piece, width), BF16),
                pltpu.VMEM((piece, width), BF16),
                pltpu.VMEM((piece, inner), BF16),
            ],
        ),
        out_shape=[
            jax.ShapeDtypeStruct((piece, width // 2), BF16),
            jax.ShapeDtypeStruct((piece, width // 2), F32),
        ],
        compiler_params=pltpu.CompilerParams(vmem_limit_bytes=VMEM_BYTES),
        cost_estimate=pl.CostEstimate(
            flops=4 * piece * inner * width,
            bytes_accessed=4 * inner * width + 12 * piece * width,
            transcendentals=piece * 256 * inner // HD,
        ),
    )(mp, base, arrived, gain, wq, ka, kb, va, vb, wo)


def body(
    hidden_in,
    database,
    neighbour_ids,
    enc_gain,
    enc_up,
    enc_down,
    dec_gain,
    w_query,
    w_key,
    w_value,
    w_out,
):
    section = lax.axis_index("section")
    mp = lax.axis_index("mp")
    tokens = hidden_in.shape[0] // 2

    entering = lax.dynamic_slice_in_dim(hidden_in, section * tokens, tokens, 0)
    encoded = encode_quarter(database, enc_gain, enc_up, enc_down)
    encoded, entering = lax.optimization_barrier((encoded, entering))
    other = swap(entering, "mp")
    state = jnp.where(
        mp == 0,
        jnp.concatenate([entering, other], axis=1),
        jnp.concatenate([other, entering], axis=1),
    )
    gains = lax.all_gather(dec_gain, "section", axis=0, tiled=True)
    wq = lax.all_gather(w_query, "section", axis=0, tiled=True)
    wk = lax.all_gather(w_key, "section", axis=0, tiled=True)
    wv = lax.all_gather(w_value, "section", axis=0, tiled=True)
    wo = lax.all_gather(w_out, "section", axis=0, tiled=True)

    normed = rms_scale(state.astype(F32), gains[0]).astype(BF16)
    q0 = (mm(normed, wq[0]) * HD ** (-0.5)).astype(BF16)
    rows_a, rows_b, q0 = fetch(encoded, neighbour_ids, q0)

    def around(layer):
        ka, va = keys_values(rows_a, wk, wv, layer)
        kb, vb = keys_values(rows_b, wk, wv, layer)
        return ka, kb, va, vb

    kv0 = around(0)
    kv1 = around(1)
    piece = tokens // CHUNKS
    mp_scalar = mp.astype(jnp.int32).reshape(1)
    sent = [first_layer(q0, kv0, wo, state, i, piece) for i in range(CHUNKS)]
    arrived = [swap(send, "mp") for send, _ in sent]
    results = []
    for i in range(CHUNKS):
        send, home = second_layer(mp_scalar, sent[i][1], arrived[i], gains[1:2], wq, kv1, wo, i)
        results.append((home + swap(send, "mp").astype(F32)).astype(BF16))
    return jnp.concatenate(results, axis=0)


def solution(mesh):
    in_specs = (
        P("db", "mp"),
        P("db", None, None),
        P(),
        P(),
        P(None, ("section", "mp")),
        P(("section", "mp"), None),
        P("section", None),
        P("section", None, "mp"),
        P("section", None, "mp"),
        P("section", None, "mp"),
        P("section", "mp", None),
    )
    out_specs = P(("db", "section"), "mp")
    return jax.shard_map(body, mesh=mesh, in_specs=in_specs, out_specs=out_specs, check_vma=False)
```

```python
import functools

import jax
import jax.numpy as jnp
from jax import lax
from jax.experimental import pallas as pl
from jax.experimental.pallas import tpu as pltpu
from jax.sharding import PartitionSpec as P

HD = 128
E = 896
NEIGH = 2
QBLOCK = 64
NBLOCK = 128
CHUNKS = 2
VMEM_BYTES = 62 << 20
F32 = jnp.float32
BF16 = jnp.bfloat16


def swap(block, axis):
    return lax.ppermute(block, axis, [(0, 1), (1, 0)])


def both_layers(own):
    other = swap(own, "section")
    first = lax.axis_index("section") == 0
    return jnp.where(first, own, other), jnp.where(first, other, own)


def rms_scale(rows_in, gain_vec):
    return (
        rows_in * lax.rsqrt(jnp.mean(rows_in * rows_in, axis=-1, keepdims=True) + 1e-06) * gain_vec
    )


def mm(a, b):
    return jnp.dot(a, b, preferred_element_type=F32)


def encode_quarter(database, enc_gain, enc_up, enc_down):
    section = lax.axis_index("section")
    mp = lax.axis_index("mp")
    held = database.shape[0]
    floats = database.reshape(-1, E).astype(F32)
    normed = rms_scale(floats, enc_gain).astype(BF16)
    inner = jax.nn.gelu(mm(normed, enc_up), approximate=True).astype(BF16)
    terms = mm(inner, enc_down).reshape(held, 2, NBLOCK // 2, E)
    mine = lax.dynamic_index_in_dim(terms, section, 1, keepdims=False)
    theirs = lax.dynamic_index_in_dim(terms, 1 - section, 1, keepdims=False)
    mine = (mine + swap(theirs, "section")).reshape(held, 2, NBLOCK // 4, E)
    away = lax.dynamic_index_in_dim(mine, 1 - mp, 1, keepdims=False)
    home = lax.dynamic_index_in_dim(mine, mp, 1, keepdims=False)
    home = home + swap(away.astype(BF16), "mp").astype(F32)
    rows = lax.dynamic_index_in_dim(
        database.reshape(held, 4, NBLOCK // 4, E), section * 2 + mp, 1, keepdims=False
    )
    return (rows.astype(F32) + home).astype(BF16)


def fetch(encoded, neighbour_ids, fill):
    section = lax.axis_index("section")
    db_count = lax.axis_size("db")
    db_index = lax.axis_index("db")
    blocks_held = encoded.shape[0]
    request = neighbour_ids.shape[0] // db_count * NEIGH
    capacity = max(2, (request + db_count - 1) // db_count)
    id_table = neighbour_ids.reshape(db_count, request)
    owners = id_table // blocks_held
    within = id_table % blocks_held
    places = jnp.arange(request)
    same_owner = owners[:, :, None] == owners[:, None, :]
    earlier = places[None, :, None] > places[None, None, :]
    rank_in = jnp.sum((same_owner & earlier).astype(jnp.int32), axis=-1)
    slot_ids = jnp.arange(capacity)
    matches = (owners[:, None, :] == db_index) & (rank_in[:, None, :] == slot_ids[None, :, None])
    send_local = jnp.sum(matches.astype(jnp.int32) * within[:, None, :], axis=-1)
    my_owner = lax.dynamic_index_in_dim(owners, db_index, 0, keepdims=False)
    my_rank = lax.dynamic_index_in_dim(rank_in, db_index, 0, keepdims=False)
    slot_pick = (my_owner * capacity + my_rank).reshape(2, request // 2)
    mine = lax.dynamic_index_in_dim(slot_pick, section, 0, keepdims=False)
    theirs = lax.dynamic_index_in_dim(slot_pick, 1 - section, 0, keepdims=False)
    payload = encoded[send_local]
    received = lax.all_to_all(payload, "db", split_axis=0, concat_axis=0, tiled=True)
    received = received.reshape(db_count * capacity, NBLOCK // 4, E)
    moved = swap(received[theirs], "section")
    groups = request // 2 // NEIGH
    near = jnp.concatenate(
        [received[mine].reshape(groups, -1, E), moved.reshape(groups, -1, E)], axis=1
    ).reshape(-1, E)
    near, fill = lax.optimization_barrier((near, fill))
    return near, swap(near, "mp"), fill


def kv_kernel(rows, wk, wv, k, v):
    k[...] = mm(rows[...], wk[0]).astype(BF16)
    v[...] = mm(rows[...], wv[0]).astype(BF16)


def keys_values(rows, wk, wv):
    count, out = rows.shape[0], wk.shape[2]
    tile = 256
    weight = pl.BlockSpec((1, E, out), lambda i: (0, 0, 0))
    made = pl.BlockSpec((tile, out), lambda i: (i, 0))
    k, v = pl.pallas_call(
        kv_kernel,
        grid=(count // tile,),
        in_specs=[pl.BlockSpec((tile, E), lambda i: (i, 0)), weight, weight],
        out_specs=[made, made],
        out_shape=[jax.ShapeDtypeStruct((count, out), BF16)] * 2,
        compiler_params=pltpu.CompilerParams(vmem_limit_bytes=VMEM_BYTES),
        cost_estimate=pl.CostEstimate(
            flops=4 * count * E * out,
            bytes_accessed=4 * E * out + 2 * count * E + 4 * count * out,
            transcendentals=0,
        ),
    )(rows, wk, wv)
    shape = (count // NBLOCK, NBLOCK, out)
    return k.reshape(shape), v.reshape(shape)


def attend_heads(q, ks, vs, blocks, heads):
    places = [(b, slice(h * HD, (h + 1) * HD)) for b in range(blocks) for h in range(heads)]
    scores = []
    for b, cols in places:
        k = jnp.concatenate([ref[b, :, cols] for ref in ks], axis=0)
        rows = slice(b * QBLOCK, (b + 1) * QBLOCK)
        scores.append(
            lax.dot_general(
                q[rows, cols], k, (((1,), (1,)), ((), ())), preferred_element_type=F32
            )
        )
    scores = jnp.concatenate(scores, axis=0)
    e = jnp.exp(scores - jnp.max(scores, axis=-1, keepdims=True))
    probs = (e / jnp.sum(e, axis=-1, keepdims=True)).astype(BF16)
    made = []
    for i, (b, cols) in enumerate(places):
        v = jnp.concatenate([ref[b, :, cols] for ref in vs], axis=0)
        made.append(mm(probs[i * QBLOCK : (i + 1) * QBLOCK], v).astype(BF16))
    rows = [jnp.concatenate(made[b * heads : (b + 1) * heads], axis=1) for b in range(blocks)]
    return jnp.concatenate(rows, axis=0)


def first_kernel(blocks, heads, q, ka, kb, va, vb, wo, state, send, base, ctx):
    @pl.when(pl.program_id(0) == 0)
    def _():
        ctx[...] = attend_heads(q[...], (ka, kb), (va, vb), blocks, heads)

    terms = mm(ctx[...], wo[0])
    send[...] = terms.astype(BF16)
    base[...] = state[...].astype(F32) + terms


def first_layer(q, kv, wo, state, part, piece):
    ka, kb, va, vb = kv
    blocks = piece // QBLOCK
    inner, width = wo.shape[1], wo.shape[2]
    tile = 1024
    around = pl.BlockSpec((blocks, NBLOCK, inner), lambda j: (part, 0, 0))
    made = pl.BlockSpec((piece, tile), lambda j: (0, j))
    return pl.pallas_call(
        functools.partial(first_kernel, blocks, inner // HD),
        grid=(width // tile,),
        in_specs=[
            pl.BlockSpec((piece, inner), lambda j: (part, 0)),
            around,
            around,
            around,
            around,
            pl.BlockSpec((1, inner, tile), lambda j: (0, 0, j)),
            pl.BlockSpec((piece, tile), lambda j: (part, j)),
        ],
        out_specs=[made, made],
        out_shape=[
            jax.ShapeDtypeStruct((piece, width), BF16),
            jax.ShapeDtypeStruct((piece, width), F32),
        ],
        scratch_shapes=[pltpu.VMEM((piece, inner), BF16)],
        compiler_params=pltpu.CompilerParams(vmem_limit_bytes=VMEM_BYTES),
        cost_estimate=pl.CostEstimate(
            flops=2 * piece * inner * (width + 512),
            bytes_accessed=2 * inner * width + 8 * piece * width,
            transcendentals=piece * 256 * inner // HD,
        ),
    )(q, ka, kb, va, vb, wo, state)


def second_kernel(
    blocks, q_steps, away, mp, base, arrived, gain, wq, ka, kb, va, vb, wo, send, home, normed, mid, ctx
):
    j = pl.program_id(0)
    q_tile = wq.shape[2]
    tile = wo.shape[2]

    @pl.when(j == 0)
    def _():
        whole = (base[...] + arrived[...].astype(F32)).astype(BF16)
        mid[...] = whole
        normed[...] = rms_scale(whole.astype(F32), gain[...]).astype(BF16)

    @pl.when(j < q_steps)
    def _():
        q = (mm(normed[...], wq[0]) * HD ** (-0.5)).astype(BF16)
        cols = pl.ds(pl.multiple_of(j * q_tile, q_tile), q_tile)
        ctx[:, cols] = attend_heads(q, (ka, kb), (va, vb), blocks, q_tile // HD)

    @pl.when((j >= q_steps) & (j < q_steps + away))
    def _():
        send[...] = mm(ctx[...], wo[0]).astype(BF16)

    @pl.when(j >= q_steps + away)
    def _():
        start = pl.multiple_of((mp[0] * away + j - q_steps - away) * tile, tile)
        home[...] = mid[:, pl.ds(start, tile)].astype(F32) + mm(ctx[...], wo[0])


def second_layer(mp, base, arrived, gain, wq, kv, wo, part):
    ka, kb, va, vb = kv
    piece, width = base.shape
    blocks = piece // QBLOCK
    inner = wo.shape[1]
    q_tile, tile = 256, 1024
    q_steps = inner // q_tile
    away = width // 2 // tile
    around = pl.BlockSpec(
        (blocks, NBLOCK, q_tile), lambda j, m: (part, 0, jnp.minimum(j, q_steps - 1))
    )
    whole = pl.BlockSpec((piece, width), lambda j, m: (0, 0))

    def out_column(j, m):
        t = jnp.maximum(j - q_steps, 0)
        return (1, 0, jnp.where(t < away, (1 - m[0]) * away + t, m[0] * away + t - away))

    return pl.pallas_call(
        functools.partial(second_kernel, blocks, q_steps, away),
        grid_spec=pltpu.PrefetchScalarGridSpec(
            num_scalar_prefetch=1,
            grid=(q_steps + 2 * away,),
            in_specs=[
                whole,
                whole,
                pl.BlockSpec((1, width), lambda j, m: (0, 0)),
                pl.BlockSpec(
                    (1, width, q_tile), lambda j, m: (1, 0, jnp.minimum(j, q_steps - 1))
                ),
                around,
                around,
                around,
                around,
                pl.BlockSpec((1, inner, tile), out_column),
            ],
            out_specs=[
                pl.BlockSpec((piece, tile), lambda j, m: (0, jnp.clip(j - q_steps, 0, away - 1))),
                pl.BlockSpec(
                    (piece, tile), lambda j, m: (0, jnp.clip(j - q_steps - away, 0, away - 1))
                ),
            ],
            scratch_shapes=[
                pltpu.VMEM((piece, width), BF16),
                pltpu.VMEM((piece, width), BF16),
                pltpu.VMEM((piece, inner), BF16),
            ],
        ),
        out_shape=[
            jax.ShapeDtypeStruct((piece, width // 2), BF16),
            jax.ShapeDtypeStruct((piece, width // 2), F32),
        ],
        compiler_params=pltpu.CompilerParams(vmem_limit_bytes=VMEM_BYTES),
        cost_estimate=pl.CostEstimate(
            flops=4 * piece * inner * width,
            bytes_accessed=4 * inner * width + 12 * piece * width,
            transcendentals=piece * 256 * inner // HD,
        ),
    )(mp, base, arrived, gain, wq, ka, kb, va, vb, wo)


def body(
    hidden_in,
    database,
    neighbour_ids,
    enc_gain,
    enc_up,
    enc_down,
    dec_gain,
    w_query,
    w_key,
    w_value,
    w_out,
):
    section = lax.axis_index("section")
    mp = lax.axis_index("mp")
    tokens = hidden_in.shape[0] // 2

    entering = lax.dynamic_slice_in_dim(hidden_in, section * tokens, tokens, 0)
    encoded = encode_quarter(database, enc_gain, enc_up, enc_down)
    encoded, entering, w_key, w_value = lax.optimization_barrier(
        (encoded, entering, w_key, w_value)
    )
    other = swap(entering, "mp")
    state = jnp.where(
        mp == 0,
        jnp.concatenate([entering, other], axis=1),
        jnp.concatenate([other, entering], axis=1),
    )
    gains = lax.all_gather(dec_gain, "section", axis=0, tiled=True)
    wq = lax.all_gather(w_query, "section", axis=0, tiled=True)
    wk = both_layers(w_key)
    wv = both_layers(w_value)
    wo = lax.all_gather(w_out, "section", axis=0, tiled=True)

    rows_a, rows_b, state = fetch(encoded, neighbour_ids, state)
    normed = rms_scale(state.astype(F32), gains[0]).astype(BF16)
    q0 = (mm(normed, wq[0]) * HD ** (-0.5)).astype(BF16)
    rows_b, q0 = lax.optimization_barrier((rows_b, q0))

    def around(layer):
        ka, va = keys_values(rows_a, wk[layer], wv[layer])
        kb, vb = keys_values(rows_b, wk[layer], wv[layer])
        return ka, kb, va, vb

    kv0 = around(0)
    kv1 = around(1)
    piece = tokens // CHUNKS
    mp_scalar = mp.astype(jnp.int32).reshape(1)
    sent = [first_layer(q0, kv0, wo, state, i, piece) for i in range(CHUNKS)]
    arrived = [swap(send, "mp") for send, _ in sent]
    results = []
    for i in range(CHUNKS):
        send, home = second_layer(mp_scalar, sent[i][1], arrived[i], gains[1:2], wq, kv1, wo, i)
        results.append((home + swap(send, "mp").astype(F32)).astype(BF16))
    return jnp.concatenate(results, axis=0)


def solution(mesh):
    in_specs = (
        P("db", "mp"),
        P("db", None, None),
        P(),
        P(),
        P(None, ("section", "mp")),
        P(("section", "mp"), None),
        P("section", None),
        P("section", None, "mp"),
        P("section", None, "mp"),
        P("section", None, "mp"),
        P("section", "mp", None),
    )
    out_specs = P(("db", "section"), "mp")
    return jax.shard_map(body, mesh=mesh, in_specs=in_specs, out_specs=out_specs, check_vma=False)
```
